32 devices in a mesh: parts: 2 (over y), frame: 4 (over z), row: 4 (over x, core).
Axes of the slice: x: 2, y: 2, z: 4, core: 2. Of those that a mesh axis runs over, the one named last changes fastest.
Arguments:
- features: bfloat16 [4, 4, 32, 32, 128], P('parts', 'frame', 'row'), parts along dimension 0, may hold values from -6 to 6
- w_in: bfloat16 [2, 3, 3, 256, 128], replicated, as said below
- b_in: float32 [2, 128], replicated, may hold values from -3 to 3
- w_mid: bfloat16 [2, 3, 3, 128, 128], replicated, may hold values from -0.1875 to 0.1875
- b_mid: float32 [2, 128], replicated, may hold values from -3 to 3
- w_out: bfloat16 [2, 3, 3, 128, 128], replicated, may hold values from -0.1875 to 0.1875
- b_out: float32 [2, 128], replicated, may hold values from -3 to 3
Outputs:
- forward_states: bfloat16 [4, 4, 32, 32, 128], P('parts', 'frame', 'row'), parts along dimension 0
- backward_states: bfloat16 [4, 4, 32, 32, 128], P('parts', 'frame', 'row'), parts along dimension 0
The draws below stay inside these ranges and needn't reach their ends.
There are 2 independent parts, one for each index of `parts`. The reference program is written for one: setup_inputs(seed, part) draws one part's arguments, and reference() takes and returns one part's arrays. A program takes and returns all parts, laid end to end along the dimension named above; an argument that names none is the same for every part. Nothing has to cross between parts.
Inputs may be any that keep to these rules, and one draw needn't show every extreme that they name: `w_in`: weights of the first convolutions.
All inputs are finite; a program needn't handle non-finite values.
Results may differ from the reference program's by a relative error of at most 0.014.
Values may be sent and summed in bfloat16 or wider, within the bound.
A program may use at most 64 MiB of HBM per device.

```python
import jax
import jax.numpy as jnp
from jax import lax

CH = 128
CLIPS = 2
COLS = 32
FRAMES = 4
ROWS = 32


def draw_w_in(key, part):
    base_key = jax.random.fold_in(key, 11)
    sign_key = jax.random.fold_in(key, 23)
    spread = (18.0 * CH) ** (-0.5)
    full_shape = (2, 3, 3, 2 * CH, CH)
    base = jnp.clip(jax.random.normal(base_key, full_shape, jnp.float32), -4.0, 4.0) * spread
    signs = (jax.random.randint(sign_key, (2, CH), 0, 2) * 2 - 1).astype(jnp.float32)
    outer = signs[:, :, None] * signs[:, None, :] * (1.8 / CH)
    padded_outer = jnp.concatenate([jnp.zeros((2, CH, CH), jnp.float32), outer], axis=1)
    return base.at[:, 1, 1].add(padded_outer).astype(jnp.bfloat16)


def block_levels(rng, shape, split, least, high):
    factor_of = 1.0
    for dim, blocks in split:
        steps = jax.random.uniform(jax.random.fold_in(jax.random.fold_in(rng, 6), dim), (blocks,), jnp.float32, least / len(split), high / len(split))
        factor_of = factor_of * jnp.repeat(jnp.exp(steps), shape[dim] // blocks).reshape((-1,) + (1,) * (len(shape) - 1 - dim))
    return factor_of


def bell_draw(key, shape, deviation, reach, cuts=(), dtype=jnp.bfloat16):
    entries = jax.random.normal(key, shape, jnp.float32) * deviation
    if len(cuts) > 0:
        entries = block_levels(key, shape, cuts, -0.22, 0.18) * entries
    return jnp.clip(entries, min=-reach, max=reach).astype(dtype)


def setup_inputs(seed: int = 0, part: int = 0) -> dict:
    streams_of = jax.random.split(jax.random.key(seed), 8)
    part_splits = jax.random.split(jax.random.fold_in(streams_of[7], part), 8)
    return {
        "features": bell_draw(part_splits[0], (CLIPS, FRAMES, ROWS, COLS, CH), 1.0, 6.0, ((1, 4), (2, 4))),
        "w_in": draw_w_in(jax.random.fold_in(streams_of[7], 71), part),
        "b_in": bell_draw(streams_of[2], (2, CH), 0.5, 3.0, (), jnp.float32),
        "w_mid": bell_draw(streams_of[3], (2, 3, 3, CH, CH), (9 * CH) ** -0.5, 0.1875),
        "b_mid": bell_draw(streams_of[4], (2, CH), 0.5, 3.0, (), jnp.float32),
        "w_out": bell_draw(streams_of[5], (2, 3, 3, CH, CH), (9 * CH) ** -0.5, 0.1875),
        "b_out": bell_draw(streams_of[6], (2, CH), 0.5, 3.0, (), jnp.float32),
    }


def pad_both(field):
    return jnp.pad(field, ((1, 1), (1, 1), (0, 0)))


def conv_layer(padded, weight, bias_vec):
    row_count = padded.shape[0] - 2
    col_count = padded.shape[1] - 2
    summed = jnp.zeros((row_count, col_count, weight.shape[-1]), jnp.float32)
    for offset_y in range(3):
        for offset_x in range(3):
            window = padded[offset_y:offset_y + row_count, offset_x:offset_x + col_count, :]
            product = jnp.dot(window.reshape(row_count * col_count, window.shape[-1]), weight[offset_y, offset_x], preferred_element_type=jnp.float32)
            summed = summed + product.reshape(row_count, col_count, weight.shape[-1])
    return summed + bias_vec


def recur_step(frame_in, carried, w_in, b_in, w_mid, b_mid, w_out, b_out):
    joined = jnp.concatenate([frame_in, carried], axis=-1)
    first_act = jax.nn.gelu(conv_layer(pad_both(joined), w_in, b_in), approximate=False).astype(jnp.bfloat16)
    middle = jax.nn.gelu(conv_layer(pad_both(first_act), w_mid, b_mid), approximate=False).astype(jnp.bfloat16)
    return (first_act.astype(jnp.float32) + conv_layer(pad_both(middle), w_out, b_out)).astype(jnp.bfloat16)


def reference(features, w_in, b_in, w_mid, b_mid, w_out, b_out):
    def one_clip(frames):
        zero_state = jnp.zeros((frames.shape[1], frames.shape[2], w_out.shape[-1]), jnp.bfloat16)

        def forward_step(carried, frame_in):
            new_state = recur_step(frame_in, carried, w_in[0], b_in[0], w_mid[0], b_mid[0], w_out[0], b_out[0])
            return new_state, new_state

        def backward_step(carried, frame_in):
            new_state = recur_step(frame_in, carried, w_in[1], b_in[1], w_mid[1], b_mid[1], w_out[1], b_out[1])
            return new_state, new_state

        _, forward_seq = lax.scan(forward_step, zero_state, frames)
        _, backward_seq = lax.scan(backward_step, zero_state, frames, reverse=True)
        return forward_seq, backward_seq

    forward_states, backward_states = lax.map(one_clip, features)
    return forward_states, backward_states
```

```python
import functools

import jax
import jax.numpy as jnp
from jax import lax
from jax.experimental import pallas as pl
from jax.experimental.pallas import tpu as pltpu
from jax.sharding import PartitionSpec as P

HALO = 3


def activate(values):
    return 0.5 * values * (lax.erf(values * (0.5**0.5)) + 1.0)


def side_taps(values, cols):
    count = values.shape[0]
    col = lax.broadcasted_iota(jnp.int32, values.shape, 0) % cols
    left = jnp.where(col == 0, 0.0, pltpu.roll(values, 1, 0))
    right = jnp.where(col == cols - 1, 0.0, pltpu.roll(values, count - 1, 0))
    return jnp.concatenate([left, values, right], axis=1).astype(jnp.bfloat16)


def conv(values, weight, cols):
    taps = side_taps(values, cols)
    out = values.shape[0] - 2 * cols
    window = jnp.concatenate([taps[dy * cols : dy * cols + out] for dy in range(3)], axis=1)
    return jnp.dot(window, weight, preferred_element_type=jnp.float32)


def in_frame(values, first_row, total_rows, cols):
    row = first_row + lax.broadcasted_iota(jnp.int32, values.shape, 0) // cols
    return jnp.where((row >= 0) & (row < total_rows), values, 0.0)


def kernel(
    frames, rows_devices,
    feat, w_in, b_in, w_mid, b_mid, w_out, b_out,
    out_f, out_b,
    halo_feat, state, pre, result, wf, ws, wm, wo,
    load_sem, feat_send, feat_recv, send_sem, recv_sem, store_sem,
):
    t = lax.axis_index("frame")
    r = lax.axis_index("row")
    clips, _, rows, cols, ch = feat.shape
    total_rows = rows * rows_devices
    span = rows + 2 * HALO
    has_up, has_down = r > 0, r < rows_devices - 1

    loads = [
        pltpu.make_async_copy(feat.at[:, 0], halo_feat.at[:, HALO : HALO + rows], load_sem.at[0]),
        pltpu.make_async_copy(w_in.at[0, :, :, :ch], wf.at[:, :, :, :ch], load_sem.at[1]),
        pltpu.make_async_copy(w_in.at[1, :, :, :ch], wf.at[:, :, :, ch:], load_sem.at[2]),
        pltpu.make_async_copy(w_mid, wm, load_sem.at[3]),
        pltpu.make_async_copy(w_out, wo, load_sem.at[4]),
        pltpu.make_async_copy(w_in.at[:, :, :, ch:], ws, load_sem.at[5]),
    ]
    for load in loads:
        load.start()

    barrier = pltpu.get_barrier_semaphore()
    near = []
    for df in (-1, 0, 1):
        for dr in (-1, 0, 1):
            if df == 0 and dr == 0:
                continue
            tt, rr = t + df, r + dr
            ok = (tt >= 0) & (tt < frames) & (rr >= 0) & (rr < rows_devices)
            near.append((ok, tt, rr))
    for ok, tt, rr in near:
        @pl.when(ok)
        def _(tt=tt, rr=rr):
            pl.semaphore_signal(barrier, inc=1, device_id={"frame": tt, "row": rr})

    @pl.when(jnp.logical_not(has_up))
    def _():
        halo_feat[:, 0:HALO] = jnp.zeros((clips, HALO, cols, ch), jnp.bfloat16)
        state[:, :, 0:HALO] = jnp.zeros((2, clips, HALO, cols, ch), jnp.bfloat16)

    @pl.when(jnp.logical_not(has_down))
    def _():
        halo_feat[:, HALO + rows :] = jnp.zeros((clips, HALO, cols, ch), jnp.bfloat16)
        state[:, :, HALO + rows :] = jnp.zeros((2, clips, HALO, cols, ch), jnp.bfloat16)

    pl.semaphore_wait(barrier, sum(jnp.where(ok, 1, 0) for ok, _, _ in near))

    feat_up = pltpu.make_async_remote_copy(
        feat.at[:, 0, 0:HALO], halo_feat.at[:, HALO + rows :],
        feat_send.at[0], feat_recv.at[0], device_id={"row": r - 1},
    )
    feat_down = pltpu.make_async_remote_copy(
        feat.at[:, 0, rows - HALO :], halo_feat.at[:, 0:HALO],
        feat_send.at[1], feat_recv.at[1], device_id={"row": r + 1},
    )
    pl.when(has_up)(feat_up.start)
    pl.when(has_down)(feat_down.start)

    for load in loads[:3]:
        load.wait()
    pl.when(has_down)(feat_up.wait_recv)
    pl.when(has_up)(feat_down.wait_recv)

    weight_f = wf[...].reshape(9 * ch, 2 * ch)
    for clip in range(clips):
        field = halo_feat[clip].reshape(span * cols, ch).astype(jnp.float32)
        both = conv(field, weight_f, cols)
        for k in range(2):
            pre[k, clip] = both[:, k * ch : (k + 1) * ch] + b_in[k : k + 1, :]
    for load in loads[3:]:
        load.wait()

    first_dir = jnp.where(2 * t >= frames, 1, 0)

    def pieces(k, clip):
        target = t + 1 - 2 * k
        source = t - 1 + 2 * k
        going = (target >= 0) & (target < frames)
        coming = (source >= 0) & (source < frames)
        made = []
        for piece, (rows_from, rows_to, dr, sends, gets) in enumerate((
            (pl.ds(0, rows), pl.ds(HALO, rows), 0, going, coming),
            (pl.ds(0, HALO), pl.ds(HALO + rows, HALO), -1, going & has_up, coming & has_down),
            (pl.ds(rows - HALO, HALO), pl.ds(0, HALO), 1, going & has_down, coming & has_up),
        )):
            copy = pltpu.make_async_remote_copy(
                result.at[k, clip, rows_from], state.at[k, clip, rows_to],
                send_sem.at[k, clip, piece], recv_sem.at[k, clip, piece],
                device_id={"frame": target, "row": r + dr},
            )
            made.append((sends, gets, copy))
        return coming, made

    def step(index, carry):
        half = index // clips
        k = first_dir + half - 2 * first_dir * half
        clip = index % clips
        coming, made = pieces(k, clip)
        for _, gets, copy in made:
            pl.when(gets)(copy.wait_recv)

        @pl.when(coming)
        def _():
            field = state[k, clip].reshape(span * cols, ch).astype(jnp.float32)
            pre[k, clip] += conv(field, ws[k].reshape(9 * ch, ch), cols)

        top = r * rows
        first = in_frame(activate(pre[k, clip]), top - 2, total_rows, cols)
        first = first.astype(jnp.bfloat16).astype(jnp.float32)
        mid = conv(first, wm[k].reshape(9 * ch, ch), cols) + b_mid[pl.ds(k, 1), :]
        mid = in_frame(activate(mid), top - 1, total_rows, cols)
        last = conv(mid, wo[k].reshape(9 * ch, ch), cols) + b_out[pl.ds(k, 1), :]
        new = first[2 * cols : (2 + rows) * cols] + last
        result[k, clip] = new.astype(jnp.bfloat16).reshape(rows, cols, ch)
        for sends, _, copy in made:
            pl.when(sends)(copy.start)

        @pl.when(k == 0)
        def _():
            pltpu.make_async_copy(result.at[0, clip], out_f.at[clip, 0], store_sem.at[0, clip]).start()

        @pl.when(k == 1)
        def _():
            pltpu.make_async_copy(result.at[1, clip], out_b.at[clip, 0], store_sem.at[1, clip]).start()

        return carry

    lax.fori_loop(0, 2 * clips, step, 0)

    pl.when(has_up)(feat_up.wait_send)
    pl.when(has_down)(feat_down.wait_send)
    for k in range(2):
        for clip in range(clips):
            for sends, _, copy in pieces(k, clip)[1]:
                pl.when(sends)(copy.wait_send)
            out = (out_f, out_b)[k]
            pltpu.make_async_copy(result.at[k, clip], out.at[clip, 0], store_sem.at[k, clip]).wait()


def on_device(features, w_in, b_in, w_mid, b_mid, w_out, b_out):
    clips, own, rows, cols, ch = features.shape
    assert own == 1 and rows >= HALO
    span = rows + 2 * HALO
    bf16 = jnp.bfloat16
    anywhere = pl.BlockSpec(memory_space=pl.ANY)
    vmem = pl.BlockSpec(memory_space=pltpu.VMEM)
    return pl.pallas_call(
        functools.partial(kernel, lax.axis_size("frame"), lax.axis_size("row")),
        out_shape=[jax.ShapeDtypeStruct(features.shape, bf16)] * 2,
        in_specs=[anywhere, anywhere, vmem, anywhere, vmem, anywhere, vmem],
        out_specs=[anywhere, anywhere],
        scratch_shapes=[
            pltpu.VMEM((clips, span, cols, ch), bf16),
            pltpu.VMEM((2, clips, span, cols, ch), bf16),
            pltpu.VMEM((2, clips, (rows + 4) * cols, ch), jnp.float32),
            pltpu.VMEM((2, clips, rows, cols, ch), bf16),
            pltpu.VMEM((3, 3, ch, 2 * ch), bf16),
            pltpu.VMEM((2, 3, 3, ch, ch), bf16),
            pltpu.VMEM((2, 3, 3, ch, ch), bf16),
            pltpu.VMEM((2, 3, 3, ch, ch), bf16),
            pltpu.SemaphoreType.DMA((6,)),
            pltpu.SemaphoreType.DMA((2,)),
            pltpu.SemaphoreType.DMA((2,)),
            pltpu.SemaphoreType.DMA((2, clips, 3)),
            pltpu.SemaphoreType.DMA((2, clips, 3)),
            pltpu.SemaphoreType.DMA((2, clips)),
        ],
        compiler_params=pltpu.CompilerParams(
            collective_id=0, has_side_effects=True, vmem_limit_bytes=32 * 1024 * 1024
        ),
    )(features, w_in, b_in, w_mid, b_mid, w_out, b_out)


def solution(mesh):
    split = P("parts", "frame", "row", None, None)
    return jax.shard_map(
        on_device,
        mesh=mesh,
        in_specs=(split, P(), P(), P(), P(), P(), P()),
        out_specs=(split, split),
        check_vma=False,
    )
```

```python
import functools

import jax
import jax.numpy as jnp
from jax import lax
from jax.experimental import pallas as pl
from jax.experimental.pallas import tpu as pltpu
from jax.sharding import PartitionSpec as P

HALO = 3


def activate(values):
    return 0.5 * values * (lax.erf(values * (0.5**0.5)) + 1.0)


def side_taps(values, cols):
    count, ch = values.shape
    col = lax.broadcasted_iota(jnp.int32, (1, cols, ch), 1)

    def beside(by, edge):
        moved = pltpu.roll(values, by, 0).reshape(count // cols, cols, ch)
        return jnp.where(col == edge, 0.0, moved).reshape(count, ch)

    left, right = beside(1, 0), beside(count - 1, cols - 1)
    return jnp.concatenate([left, values, right], axis=1).astype(jnp.bfloat16)


def conv(values, weight, cols):
    taps = side_taps(values, cols)
    out = values.shape[0] - 2 * cols
    window = jnp.concatenate([taps[dy * cols : dy * cols + out] for dy in range(3)], axis=1)
    return jnp.dot(window, weight, preferred_element_type=jnp.float32)


def in_frame(values, rim, has_up, has_down):
    upper = jnp.where(has_up, values[:rim], 0.0)
    lower = jnp.where(has_down, values[-rim:], 0.0)
    return jnp.concatenate([upper, values[rim:-rim], lower], axis=0)


def kernel(
    frames, rows_devices,
    feat, w_in, b_in_hbm, w_mid, b_mid_hbm, w_out, b_out_hbm,
    out_f, out_b,
    halo_feat, state, pre, result, wf, ws, wm, wo, b_in, b_mid, b_out,
    load_sem, feat_send, feat_recv, send_sem, recv_sem, store_sem,
):
    t = lax.axis_index("frame")
    r = lax.axis_index("row")
    clips, _, rows, cols, ch = feat.shape
    span = rows + 2 * HALO
    has_up, has_down = r > 0, r < rows_devices - 1

    loads = [
        pltpu.make_async_copy(feat.at[:, 0], halo_feat.at[:, HALO : HALO + rows], load_sem.at[0]),
        pltpu.make_async_copy(w_in.at[0, :, :, :ch], wf.at[:, :, :, :ch], load_sem.at[1]),
        pltpu.make_async_copy(w_in.at[1, :, :, :ch], wf.at[:, :, :, ch:], load_sem.at[2]),
        pltpu.make_async_copy(b_in_hbm, b_in, load_sem.at[6]),
        pltpu.make_async_copy(w_mid, wm, load_sem.at[3]),
        pltpu.make_async_copy(w_out, wo, load_sem.at[4]),
        pltpu.make_async_copy(w_in.at[:, :, :, ch:], ws, load_sem.at[5]),
        pltpu.make_async_copy(b_mid_hbm, b_mid, load_sem.at[7]),
        pltpu.make_async_copy(b_out_hbm, b_out, load_sem.at[8]),
    ]
    for load in loads:
        load.start()

    barrier = pltpu.get_barrier_semaphore()
    near = []
    for df in (-1, 0, 1):
        for dr in (-1, 0, 1):
            if df == 0 and dr == 0:
                continue
            tt, rr = t + df, r + dr
            ok = (tt >= 0) & (tt < frames) & (rr >= 0) & (rr < rows_devices)
            near.append((ok, tt, rr))
    for ok, tt, rr in near:
        @pl.when(ok)
        def _(tt=tt, rr=rr):
            pl.semaphore_signal(barrier, inc=1, device_id={"frame": tt, "row": rr})

    @pl.when(jnp.logical_not(has_up))
    def _():
        halo_feat[:, 0:HALO] = jnp.zeros((clips, HALO, cols, ch), jnp.bfloat16)
        state[:, :, 0:HALO] = jnp.zeros((2, clips, HALO, cols, ch), jnp.bfloat16)

    @pl.when(jnp.logical_not(has_down))
    def _():
        halo_feat[:, HALO + rows :] = jnp.zeros((clips, HALO, cols, ch), jnp.bfloat16)
        state[:, :, HALO + rows :] = jnp.zeros((2, clips, HALO, cols, ch), jnp.bfloat16)

    pl.semaphore_wait(barrier, sum(jnp.where(ok, 1, 0) for ok, _, _ in near))

    feat_up = pltpu.make_async_remote_copy(
        feat.at[:, 0, 0:HALO], halo_feat.at[:, HALO + rows :],
        feat_send.at[0], feat_recv.at[0], device_id={"row": r - 1},
    )
    feat_down = pltpu.make_async_remote_copy(
        feat.at[:, 0, rows - HALO :], halo_feat.at[:, 0:HALO],
        feat_send.at[1], feat_recv.at[1], device_id={"row": r + 1},
    )
    pl.when(has_up)(feat_up.start)
    pl.when(has_down)(feat_down.start)

    for load in loads[:4]:
        load.wait()
    pl.when(has_down)(feat_up.wait_recv)
    pl.when(has_up)(feat_down.wait_recv)

    weight_f = wf[...].reshape(9 * ch, 2 * ch)
    for clip in range(clips):
        field = halo_feat[clip].reshape(span * cols, ch).astype(jnp.float32)
        both = conv(field, weight_f, cols)
        for k in range(2):
            pre[k, clip] = both[:, k * ch : (k + 1) * ch] + b_in[k : k + 1, :]
    for load in loads[4:]:
        load.wait()

    first_dir = jnp.where(2 * t >= frames, 1, 0)

    def pieces(k, clip):
        target = t + 1 - 2 * k
        source = t - 1 + 2 * k
        going = (target >= 0) & (target < frames)
        coming = (source >= 0) & (source < frames)
        made = []
        for piece, (rows_from, rows_to, dr, sends, gets) in enumerate((
            (pl.ds(0, rows), pl.ds(HALO, rows), 0, going, coming),
            (pl.ds(0, HALO), pl.ds(HALO + rows, HALO), -1, going & has_up, coming & has_down),
            (pl.ds(rows - HALO, HALO), pl.ds(0, HALO), 1, going & has_down, coming & has_up),
        )):
            copy = pltpu.make_async_remote_copy(
                result.at[k, clip, rows_from], state.at[k, clip, rows_to],
                send_sem.at[k, clip, piece], recv_sem.at[k, clip, piece],
                device_id={"frame": target, "row": r + dr},
            )
            made.append((sends, gets, copy))
        return coming, made

    def step(index, carry):
        half = index // clips
        k = first_dir + half - 2 * first_dir * half
        clip = index % clips
        coming, made = pieces(k, clip)
        for _, gets, copy in made:
            pl.when(gets)(copy.wait_recv)

        @pl.when(coming)
        def _():
            field = state[k, clip].reshape(span * cols, ch).astype(jnp.float32)
            pre[k, clip] += conv(field, ws[k].reshape(9 * ch, ch), cols)

        first = in_frame(activate(pre[k, clip]), 2 * cols, has_up, has_down)
        first = first.astype(jnp.bfloat16).astype(jnp.float32)
        mid = conv(first, wm[k].reshape(9 * ch, ch), cols) + b_mid[pl.ds(k, 1), :]
        mid = in_frame(activate(mid), cols, has_up, has_down)
        last = conv(mid, wo[k].reshape(9 * ch, ch), cols) + b_out[pl.ds(k, 1), :]
        new = first[2 * cols : (2 + rows) * cols] + last
        result[k, clip] = new.astype(jnp.bfloat16).reshape(rows, cols, ch)
        for sends, _, copy in made:
            pl.when(sends)(copy.start)

        @pl.when(k == 0)
        def _():
            pltpu.make_async_copy(result.at[0, clip], out_f.at[clip, 0], store_sem.at[0, clip]).start()

        @pl.when(k == 1)
        def _():
            pltpu.make_async_copy(result.at[1, clip], out_b.at[clip, 0], store_sem.at[1, clip]).start()

        return carry

    lax.fori_loop(0, 2 * clips, step, 0)

    pl.when(has_up)(feat_up.wait_send)
    pl.when(has_down)(feat_down.wait_send)
    for k in range(2):
        for clip in range(clips):
            for sends, _, copy in pieces(k, clip)[1]:
                pl.when(sends)(copy.wait_send)
            out = (out_f, out_b)[k]
            pltpu.make_async_copy(result.at[k, clip], out.at[clip, 0], store_sem.at[k, clip]).wait()


def on_device(features, w_in, b_in, w_mid, b_mid, w_out, b_out):
    clips, own, rows, cols, ch = features.shape
    assert own == 1 and rows >= HALO
    span = rows + 2 * HALO
    bf16 = jnp.bfloat16
    hbm = pl.BlockSpec(memory_space=pltpu.HBM)
    return pl.pallas_call(
        functools.partial(kernel, lax.axis_size("frame"), lax.axis_size("row")),
        out_shape=[jax.ShapeDtypeStruct(features.shape, bf16)] * 2,
        in_specs=[hbm] * 7,
        out_specs=[hbm, hbm],
        scratch_shapes=[
            pltpu.VMEM((clips, span, cols, ch), bf16),
            pltpu.VMEM((2, clips, span, cols, ch), bf16),
            pltpu.VMEM((2, clips, (rows + 4) * cols, ch), jnp.float32),
            pltpu.VMEM((2, clips, rows, cols, ch), bf16),
            pltpu.VMEM((3, 3, ch, 2 * ch), bf16),
            pltpu.VMEM((2, 3, 3, ch, ch), bf16),
            pltpu.VMEM((2, 3, 3, ch, ch), bf16),
            pltpu.VMEM((2, 3, 3, ch, ch), bf16),
            pltpu.VMEM((2, ch), jnp.float32),
            pltpu.VMEM((2, ch), jnp.float32),
            pltpu.VMEM((2, ch), jnp.float32),
            pltpu.SemaphoreType.DMA((9,)),
            pltpu.SemaphoreType.DMA((2,)),
            pltpu.SemaphoreType.DMA((2,)),
            pltpu.SemaphoreType.DMA((2, clips, 3)),
            pltpu.SemaphoreType.DMA((2, clips, 3)),
            pltpu.SemaphoreType.DMA((2, clips)),
        ],
        compiler_params=pltpu.CompilerParams(
            collective_id=0, has_side_effects=True, vmem_limit_bytes=32 * 1024 * 1024
        ),
    )(features, w_in, b_in, w_mid, b_mid, w_out, b_out)


def solution(mesh):
    split = P("parts", "frame", "row", None, None)
    return jax.shard_map(
        on_device,
        mesh=mesh,
        in_specs=(split, P(), P(), P(), P(), P(), P()),
        out_specs=(split, split),
        check_vma=False,
    )
```

```python
import functools

import jax
import jax.numpy as jnp
from jax import lax
from jax.experimental import pallas as pl
from jax.experimental.pallas import tpu as pltpu
from jax.sharding import PartitionSpec as P

HALO = 3


def activate(values):
    return 0.5 * values * (lax.erf(values * (0.5**0.5)) + 1.0)


def side_taps(values, cols):
    count, ch = values.shape
    col = lax.broadcasted_iota(jnp.int32, (1, cols, ch), 1)

    def beside(by, edge):
        moved = pltpu.roll(values, by, 0).reshape(count // cols, cols, ch)
        return jnp.where(col == edge, 0.0, moved).reshape(count, ch)

    left, right = beside(1, 0), beside(count - 1, cols - 1)
    return jnp.concatenate([left, values, right], axis=1).astype(jnp.bfloat16)


def conv(values, weight, cols):
    taps = side_taps(values, cols)
    out = values.shape[0] - 2 * cols
    window = jnp.concatenate([taps[dy * cols : dy * cols + out] for dy in range(3)], axis=1)
    return jnp.dot(window, weight, preferred_element_type=jnp.float32)


def in_frame(values, rim, has_up, has_down):
    upper = jnp.where(has_up, values[:rim], 0.0)
    lower = jnp.where(has_down, values[-rim:], 0.0)
    return jnp.concatenate([upper, values[rim:-rim], lower], axis=0)


def kernel(
    frames, rows_devices,
    feat, w_in, b_in_hbm, w_mid, b_mid_hbm, w_out, b_out_hbm,
    out_f, out_b,
    fields, state, pre, wi, wm, wo, b_in, b_mid, b_out,
    load_sem, feat_send, feat_recv, first_send, rim_send, rim_recv,
    state_send, state_recv, out_send, out_recv,
):
    z = lax.axis_index("frame")
    r = lax.axis_index("row")
    clips, _, rows, cols, ch = feat.shape
    span = rows + 2 * HALO
    has_up, has_down = r > 0, r < rows_devices - 1
    own = pl.ds(HALO, rows)
    sides = (
        (has_up, -1, 0, HALO + rows),
        (has_down, 1, rows - HALO, 0),
    )

    back = jnp.where(z >= frames - clips, 1, 0)
    clip = z + back * (frames - 1 - 2 * z)
    is_host = (z < clips) | (z >= frames - clips)

    def host_of(k, c):
        return c + k * (frames - 1 - 2 * c)

    def frame_of(s):
        return s + back * (frames - 1 - 2 * s)

    loads = [
        pltpu.make_async_copy(w_in.at[back], wi, load_sem.at[0]),
        pltpu.make_async_copy(b_in_hbm, b_in, load_sem.at[1]),
        pltpu.make_async_copy(w_mid.at[back], wm, load_sem.at[2]),
        pltpu.make_async_copy(b_mid_hbm, b_mid, load_sem.at[3]),
        pltpu.make_async_copy(w_out.at[back], wo, load_sem.at[4]),
        pltpu.make_async_copy(b_out_hbm, b_out, load_sem.at[5]),
    ]
    for load in loads:
        load.start()

    barrier = pltpu.get_barrier_semaphore()
    near = [(z != zz, zz, r) for zz in range(frames)]
    for near_row, offset, _, _ in sides:
        for dz in (-1, 0, 1):
            near.append((near_row & (z + dz >= 0) & (z + dz < frames), z + dz, r + offset))
    for ok, zz, rr in near:
        @pl.when(ok)
        def _(zz=zz, rr=rr):
            pl.semaphore_signal(barrier, inc=1, device_id={"frame": zz, "row": rr})

    for near_row, _, _, keep in sides:
        at = HALO + rows - keep
        @pl.when(jnp.logical_not(near_row))
        def _(at=at):
            zeros = jnp.zeros((frames, HALO, cols, ch), jnp.bfloat16)
            fields[:, at : at + HALO] = zeros
            state[:, at : at + HALO] = zeros

    pl.semaphore_wait(barrier, sum(jnp.where(ok, 1, 0) for ok, _, _ in near))

    late = jnp.where(2 * z >= frames, 1, 0)

    def feature_copy(i):
        half = i // clips
        k = late + half - 2 * late * half
        c = i % clips
        host = host_of(k, c)
        copy = pltpu.make_async_remote_copy(
            feat.at[c, 0], fields.at[z, own], feat_send.at[i], feat_recv.at[z],
            device_id={"frame": host},
        )
        return c, host, copy

    def first_rims(c):
        host = host_of(back, c)
        is_first = (z == 0) | (z == frames - 1)
        return [
            (
                is_first & near_row,
                pltpu.make_async_remote_copy(
                    feat.at[c, 0, pl.ds(take, HALO)], fields.at[z, pl.ds(keep, HALO)],
                    first_send.at[c, side], rim_recv.at[z, side],
                    device_id={"frame": host, "row": r + offset},
                ),
            )
            for side, (near_row, offset, take, keep) in enumerate(sides)
        ]

    for i in range(2 * clips):
        c, host, copy = feature_copy(i)
        pl.when(host != z)(copy.start)
        @pl.when(host == z)
        def _(c=c):
            pltpu.make_async_copy(feat.at[c, 0], fields.at[z, own], feat_recv.at[z]).start()
        if i < clips:
            for ok, copy in first_rims(i):
                pl.when(ok)(copy.start)

    def rim_copies(buffer, index, sends, gets):
        made = []
        for side, (near_row, offset, take, keep) in enumerate(sides):
            copy = pltpu.make_async_remote_copy(
                buffer.at[index, pl.ds(HALO + take, HALO)], buffer.at[index, pl.ds(keep, HALO)],
                sends.at[index, side], gets.at[index, side], device_id={"row": r + offset},
            )
            made.append((near_row, sides[1 - side][0], copy))
        return made

    def field_rims(f):
        return rim_copies(fields, f, rim_send, rim_recv)

    def state_rims(s):
        return rim_copies(state, s, state_send, state_recv)

    def wait_field(f):
        pltpu.make_async_copy(feat.at[0, 0], fields.at[f, own], feat_recv.at[f]).wait()

    def wait_rims(copies):
        for _, comes, copy in copies:
            pl.when(comes)(copy.wait_recv)

    def out_copy(s, k):
        return pltpu.make_async_remote_copy(
            state.at[s, own], (out_f, out_b)[k].at[clip, 0], out_send.at[s],
            out_recv.at[k, clip], device_id={"frame": frame_of(s)},
        )

    def features_part(f):
        field = fields[f].reshape(span * cols, ch).astype(jnp.float32)
        pre[...] = conv(field, wi[:, :, :ch].reshape(9 * ch, ch), cols) + b_in[pl.ds(back, 1), :]

    def chain():
        wait_field(frame_of(0))
        for load in loads[:2]:
            load.wait()
        wait_rims(field_rims(frame_of(0)))
        features_part(frame_of(0))
        for load in loads[2:]:
            load.wait()

        def step(s, carry):
            f = frame_of(s)
            more = s < frames - 1
            then = frame_of(jnp.minimum(s + 1, frames - 1))

            @pl.when(more)
            def _():
                wait_field(then)
                for goes, _, copy in field_rims(then):
                    pl.when(goes)(copy.start)

            @pl.when(s > 0)
            def _():
                before = jnp.maximum(s - 1, 0)
                wait_rims(state_rims(before))
                field = state[before].reshape(span * cols, ch).astype(jnp.float32)
                pre[...] += conv(field, wi[:, :, ch:].reshape(9 * ch, ch), cols)

            first = in_frame(activate(pre[...]), 2 * cols, has_up, has_down)
            first = first.astype(jnp.bfloat16).astype(jnp.float32)
            mid = conv(first, wm[...].reshape(9 * ch, ch), cols) + b_mid[pl.ds(back, 1), :]
            mid = in_frame(activate(mid), cols, has_up, has_down)
            last = conv(mid, wo[...].reshape(9 * ch, ch), cols) + b_out[pl.ds(back, 1), :]
            new = first[2 * cols : (2 + rows) * cols] + last
            state[s, own] = new.astype(jnp.bfloat16).reshape(rows, cols, ch)

            for goes, _, copy in state_rims(s):
                pl.when(goes & more)(copy.start)
            for k in range(2):
                pl.when((back == k) & (f != z))(out_copy(s, k).start)
                @pl.when((back == k) & (f == z))
                def _(k=k):
                    pltpu.make_async_copy(
                        state.at[s, own], (out_f, out_b)[k].at[clip, 0], out_recv.at[k, clip]
                    ).start()

            @pl.when(more)
            def _():
                wait_rims(field_rims(then))
                features_part(then)

            return carry

        lax.fori_loop(0, frames, step, 0)

        for s in range(frames):
            f = frame_of(s)
            pl.when(f != z)(out_copy(s, 0).wait_send)
            if s < frames - 1:
                for goes, _, copy in state_rims(s):
                    pl.when(goes)(copy.wait_send)
            if s > 0:
                for goes, _, copy in field_rims(f):
                    pl.when(goes)(copy.wait_send)

    if frames == 2 * clips:
        chain()
    else:
        pl.when(is_host)(chain)
        @pl.when(jnp.logical_not(is_host))
        def _():
            for load in loads:
                load.wait()

    for i in range(2 * clips):
        _, host, copy = feature_copy(i)
        pl.when(host != z)(copy.wait_send)
    for c in range(clips):
        for ok, copy in first_rims(c):
            pl.when(ok)(copy.wait_send)
        for k, out in enumerate((out_f, out_b)):
            pltpu.make_async_copy(state.at[0, own], out.at[c, 0], out_recv.at[k, c]).wait()


def on_device(features, w_in, b_in, w_mid, b_mid, w_out, b_out):
    clips, held, rows, cols, ch = features.shape
    frames = lax.axis_size("frame")
    assert held == 1 and rows >= HALO and clips <= 2 and frames >= 2 * clips
    span = rows + 2 * HALO
    bf16 = jnp.bfloat16
    hbm = pl.BlockSpec(memory_space=pltpu.HBM)
    dma = pltpu.SemaphoreType.DMA
    return pl.pallas_call(
        functools.partial(kernel, frames, lax.axis_size("row")),
        out_shape=[jax.ShapeDtypeStruct(features.shape, bf16)] * 2,
        in_specs=[hbm] * 7,
        out_specs=[hbm, hbm],
        scratch_shapes=[
            pltpu.VMEM((frames, span, cols, ch), bf16),
            pltpu.VMEM((frames, span, cols, ch), bf16),
            pltpu.VMEM(((rows + 4) * cols, ch), jnp.float32),
            pltpu.VMEM((3, 3, 2 * ch, ch), bf16),
            pltpu.VMEM((3, 3, ch, ch), bf16),
            pltpu.VMEM((3, 3, ch, ch), bf16),
            pltpu.VMEM((2, ch), jnp.float32),
            pltpu.VMEM((2, ch), jnp.float32),
            pltpu.VMEM((2, ch), jnp.float32),
            dma((6,)),
            dma((2 * clips,)),
            dma((frames,)),
            dma((clips, 2)),
            dma((frames, 2)),
            dma((frames, 2)),
            dma((frames, 2)),
            dma((frames, 2)),
            dma((frames,)),
            dma((2, clips)),
        ],
        compiler_params=pltpu.CompilerParams(
            collective_id=0, has_side_effects=True, vmem_limit_bytes=60 * 1024 * 1024
        ),
    )(features, w_in, b_in, w_mid, b_mid, w_out, b_out)


def solution(mesh):
    split = P("parts", "frame", "row", None, None)
    return jax.shard_map(
        on_device,
        mesh=mesh,
        in_specs=(split, P(), P(), P(), P(), P(), P()),
        out_specs=(split, split),
        check_vma=False,
    )
```

```python
import functools

import jax
import jax.numpy as jnp
from jax import lax
from jax.experimental import pallas as pl
from jax.experimental.pallas import tpu as pltpu
from jax.sharding import PartitionSpec as P

HALO = 3


def activate(values):
    return 0.5 * values * (lax.erf(values * (0.5**0.5)) + 1.0)


def side_taps(values, cols):
    count, ch = values.shape
    col = lax.broadcasted_iota(jnp.int32, (1, cols, ch), 1)

    def beside(by, edge):
        moved = pltpu.roll(values, by, 0).reshape(count // cols, cols, ch)
        return jnp.where(col == edge, 0.0, moved).reshape(count, ch)

    left, right = beside(1, 0), beside(count - 1, cols - 1)
    return jnp.concatenate([left, values, right], axis=1).astype(jnp.bfloat16)


def conv(values, weight, cols):
    taps = side_taps(values, cols)
    ch = values.shape[1]
    window = jnp.concatenate([taps[:-cols], taps[cols:]], axis=1)
    weight = weight[...].reshape(6 * ch, 2 * ch)
    both = jnp.dot(window, weight, preferred_element_type=jnp.float32)
    return both[cols:, :ch] + both[:-cols, ch:]


def paired(source, target, sem):
    ch = source.shape[-1]
    return [
        pltpu.make_async_copy(source.at[pl.ds(1, 2)], target.at[:, :, :, :ch], sem.at[0]),
        pltpu.make_async_copy(source.at[0], target.at[0, :, :, ch:], sem.at[1]),
    ]


def in_frame(values, rim, has_up, has_down):
    upper = jnp.where(has_up, values[:rim], 0.0)
    lower = jnp.where(has_down, values[-rim:], 0.0)
    return jnp.concatenate([upper, values[rim:-rim], lower], axis=0)


def kernel(
    frames, rows_devices,
    feat, w_in, b_in_hbm, w_mid, b_mid_hbm, w_out, b_out_hbm,
    out_f, out_b,
    fields, state, pre, wf, ws, wm, wo, b_in, b_mid, b_out,
    load_sem, bias_sem, feat_send, feat_recv, first_send, rim_send, rim_recv,
    state_send, state_recv, out_send, out_recv,
):
    z = lax.axis_index("frame")
    r = lax.axis_index("row")
    clips, _, rows, cols, ch = feat.shape
    span = rows + 2 * HALO
    has_up, has_down = r > 0, r < rows_devices - 1
    own = pl.ds(HALO, rows)
    sides = (
        (has_up, -1, 0, HALO + rows),
        (has_down, 1, rows - HALO, 0),
    )

    back = jnp.where(z >= frames - clips, 1, 0)
    clip = z + back * (frames - 1 - 2 * z)
    is_host = (z < clips) | (z >= frames - clips)

    def host_of(k, c):
        return c + k * (frames - 1 - 2 * c)

    def frame_of(s):
        return s + back * (frames - 1 - 2 * s)

    weights = (
        (w_in.at[back, :, :, :ch], wf),
        (w_in.at[back, :, :, ch:], ws),
        (w_mid.at[back], wm),
        (w_out.at[back], wo),
    )
    loads = []
    for i, (source, target) in enumerate(weights):
        loads += paired(source, target, load_sem.at[i])
    biases = ((b_in_hbm, b_in), (b_mid_hbm, b_mid), (b_out_hbm, b_out))
    for i, (source, target) in enumerate(biases):
        loads.insert(2 + i, pltpu.make_async_copy(source, target, bias_sem.at[i]))
    for load in loads:
        load.start()
    for _, target in weights:
        target[1, :, :, ch:] = jnp.zeros((3, ch, ch), jnp.bfloat16)

    barrier = pltpu.get_barrier_semaphore()
    near = [(z != zz, zz, r) for zz in range(frames)]
    for near_row, offset, _, _ in sides:
        for dz in (-1, 0, 1):
            near.append((near_row & (z + dz >= 0) & (z + dz < frames), z + dz, r + offset))
    for ok, zz, rr in near:
        @pl.when(ok)
        def _(zz=zz, rr=rr):
            pl.semaphore_signal(barrier, inc=1, device_id={"frame": zz, "row": rr})

    for near_row, _, _, keep in sides:
        at = HALO + rows - keep
        @pl.when(jnp.logical_not(near_row))
        def _(at=at):
            zeros = jnp.zeros((frames, HALO, cols, ch), jnp.bfloat16)
            fields[:, at : at + HALO] = zeros
            state[:, at : at + HALO] = zeros

    pl.semaphore_wait(barrier, sum(jnp.where(ok, 1, 0) for ok, _, _ in near))

    late = jnp.where(2 * z >= frames, 1, 0)

    def feature_copy(i):
        half = i // clips
        k = late + half - 2 * late * half
        c = i % clips
        host = host_of(k, c)
        copy = pltpu.make_async_remote_copy(
            feat.at[c, 0], fields.at[z, own], feat_send.at[i], feat_recv.at[z],
            device_id={"frame": host},
        )
        return c, host, copy

    def first_rims(c):
        host = host_of(back, c)
        is_first = (z == 0) | (z == frames - 1)
        return [
            (
                is_first & near_row,
                pltpu.make_async_remote_copy(
                    feat.at[c, 0, pl.ds(take, HALO)], fields.at[z, pl.ds(keep, HALO)],
                    first_send.at[c, side], rim_recv.at[z, side],
                    device_id={"frame": host, "row": r + offset},
                ),
            )
            for side, (near_row, offset, take, keep) in enumerate(sides)
        ]

    for i in range(2 * clips):
        c, host, copy = feature_copy(i)
        pl.when(host != z)(copy.start)
        @pl.when(host == z)
        def _(c=c):
            pltpu.make_async_copy(feat.at[c, 0], fields.at[z, own], feat_recv.at[z]).start()
        if i < clips:
            for ok, copy in first_rims(i):
                pl.when(ok)(copy.start)

    def rim_copies(buffer, index, sends, gets):
        made = []
        for side, (near_row, offset, take, keep) in enumerate(sides):
            copy = pltpu.make_async_remote_copy(
                buffer.at[index, pl.ds(HALO + take, HALO)], buffer.at[index, pl.ds(keep, HALO)],
                sends.at[index, side], gets.at[index, side], device_id={"row": r + offset},
            )
            made.append((near_row, sides[1 - side][0], copy))
        return made

    def field_rims(f):
        return rim_copies(fields, f, rim_send, rim_recv)

    def state_rims(s):
        return rim_copies(state, s, state_send, state_recv)

    def wait_field(f):
        pltpu.make_async_copy(feat.at[0, 0], fields.at[f, own], feat_recv.at[f]).wait()

    def wait_rims(copies):
        for _, comes, copy in copies:
            pl.when(comes)(copy.wait_recv)

    def out_copy(s, k):
        return pltpu.make_async_remote_copy(
            state.at[s, own], (out_f, out_b)[k].at[clip, 0], out_send.at[s],
            out_recv.at[k, clip], device_id={"frame": frame_of(s)},
        )

    def features_part(f):
        field = fields[f].reshape(span * cols, ch).astype(jnp.float32)
        pre[...] = conv(field, wf, cols) + b_in[pl.ds(back, 1), :]

    def chain():
        wait_field(frame_of(0))
        for load in loads[:5]:
            load.wait()
        wait_rims(field_rims(frame_of(0)))
        features_part(frame_of(0))
        for load in loads[5:]:
            load.wait()

        def step(s, carry):
            f = frame_of(s)
            more = s < frames - 1
            then = frame_of(jnp.minimum(s + 1, frames - 1))

            @pl.when(more)
            def _():
                wait_field(then)
                for goes, _, copy in field_rims(then):
                    pl.when(goes)(copy.start)

            @pl.when(s > 0)
            def _():
                before = jnp.maximum(s - 1, 0)
                wait_rims(state_rims(before))
                field = state[before].reshape(span * cols, ch).astype(jnp.float32)
                pre[...] += conv(field, ws, cols)

            first = in_frame(activate(pre[...]), 2 * cols, has_up, has_down)
            first = first.astype(jnp.bfloat16).astype(jnp.float32)
            mid = conv(first, wm, cols) + b_mid[pl.ds(back, 1), :]
            mid = in_frame(activate(mid), cols, has_up, has_down)
            last = conv(mid, wo, cols) + b_out[pl.ds(back, 1), :]
            new = first[2 * cols : (2 + rows) * cols] + last
            state[s, own] = new.astype(jnp.bfloat16).reshape(rows, cols, ch)

            for goes, _, copy in state_rims(s):
                pl.when(goes & more)(copy.start)
            for k in range(2):
                pl.when((back == k) & (f != z))(out_copy(s, k).start)
                @pl.when((back == k) & (f == z))
                def _(k=k):
                    pltpu.make_async_copy(
                        state.at[s, own], (out_f, out_b)[k].at[clip, 0], out_recv.at[k, clip]
                    ).start()

            @pl.when(more)
            def _():
                wait_rims(field_rims(then))
                features_part(then)

            return carry

        lax.fori_loop(0, frames, step, 0)

        for s in range(frames):
            f = frame_of(s)
            pl.when(f != z)(out_copy(s, 0).wait_send)
            if s < frames - 1:
                for goes, _, copy in state_rims(s):
                    pl.when(goes)(copy.wait_send)
            if s > 0:
                for goes, _, copy in field_rims(f):
                    pl.when(goes)(copy.wait_send)

    if frames == 2 * clips:
        chain()
    else:
        pl.when(is_host)(chain)
        @pl.when(jnp.logical_not(is_host))
        def _():
            for load in loads:
                load.wait()

    for i in range(2 * clips):
        _, host, copy = feature_copy(i)
        pl.when(host != z)(copy.wait_send)
    for c in range(clips):
        for ok, copy in first_rims(c):
            pl.when(ok)(copy.wait_send)
        for k, out in enumerate((out_f, out_b)):
            pltpu.make_async_copy(state.at[0, own], out.at[c, 0], out_recv.at[k, c]).wait()


def finish(held_f, held_b, out_f, out_b, sem):
    copies = [
        pltpu.make_async_copy(held_f, out_f, sem.at[0]),
        pltpu.make_async_copy(held_b, out_b, sem.at[1]),
    ]
    for copy in copies:
        copy.start()
    for copy in copies:
        copy.wait()


def on_device(features, w_in, b_in, w_mid, b_mid, w_out, b_out):
    clips, held, rows, cols, ch = features.shape
    frames = lax.axis_size("frame")
    assert held == 1 and rows >= HALO and clips <= 2 and frames >= 2 * clips
    span = rows + 2 * HALO
    bf16 = jnp.bfloat16
    hbm = pl.BlockSpec(memory_space=pltpu.HBM)
    dma = pltpu.SemaphoreType.DMA
    states = pl.pallas_call(
        functools.partial(kernel, frames, lax.axis_size("row")),
        out_shape=[jax.ShapeDtypeStruct(features.shape, bf16)] * 2,
        in_specs=[hbm] * 7,
        out_specs=[hbm, hbm],
        scratch_shapes=[
            pltpu.VMEM((frames, span, cols, ch), bf16),
            pltpu.VMEM((frames, span, cols, ch), bf16),
            pltpu.VMEM(((rows + 4) * cols, ch), jnp.float32),
            pltpu.VMEM((2, 3, ch, 2 * ch), bf16),
            pltpu.VMEM((2, 3, ch, 2 * ch), bf16),
            pltpu.VMEM((2, 3, ch, 2 * ch), bf16),
            pltpu.VMEM((2, 3, ch, 2 * ch), bf16),
            pltpu.VMEM((2, ch), jnp.float32),
            pltpu.VMEM((2, ch), jnp.float32),
            pltpu.VMEM((2, ch), jnp.float32),
            dma((4, 2)),
            dma((3,)),
            dma((2 * clips,)),
            dma((frames,)),
            dma((clips, 2)),
            dma((frames, 2)),
            dma((frames, 2)),
            dma((frames, 2)),
            dma((frames, 2)),
            dma((frames,)),
            dma((2, clips)),
        ],
        compiler_params=pltpu.CompilerParams(
            collective_id=0, has_side_effects=True, vmem_limit_bytes=60 * 1024 * 1024
        ),
    )(features, w_in, b_in, w_mid, b_mid, w_out, b_out)
    return pl.pallas_call(
        finish,
        out_shape=[jax.ShapeDtypeStruct(features.shape, bf16)] * 2,
        in_specs=[pl.BlockSpec(memory_space=pl.ANY)] * 2,
        out_specs=[hbm, hbm],
        scratch_shapes=[dma((2,))],
        compiler_params=pltpu.CompilerParams(vmem_limit_bytes=60 * 1024 * 1024),
    )(*states)


def solution(mesh):
    split = P("parts", "frame", "row", None, None)
    return jax.shard_map(
        on_device,
        mesh=mesh,
        in_specs=(split, P(), P(), P(), P(), P(), P()),
        out_specs=(split, split),
        check_vma=False,
    )
```

```python
import functools

import jax
import jax.numpy as jnp
from jax import lax
from jax.experimental import pallas as pl
from jax.experimental.pallas import tpu as pltpu
from jax.sharding import PartitionSpec as P

HALO = 3


def activate(values):
    return 0.5 * values * (lax.erf(values * (0.5**0.5)) + 1.0)


def side_taps(values, cols):
    count, ch = values.shape
    col = lax.broadcasted_iota(jnp.int32, (1, cols, ch), 1)

    def beside(by, edge):
        moved = pltpu.roll(values, by, 0).reshape(count // cols, cols, ch)
        return jnp.where(col == edge, 0.0, moved).reshape(count, ch)

    left, right = beside(1, 0), beside(count - 1, cols - 1)
    return jnp.concatenate([left, values, right], axis=1).astype(jnp.bfloat16)


def conv(fields, weight, cols):
    ch = fields[0].shape[1]
    taps = [side_taps(field, cols) for field in fields]
    windows = [jnp.concatenate([tap[:-cols], tap[cols:]], axis=1) for tap in taps]
    window = windows[0] if len(windows) == 1 else jnp.concatenate(windows, axis=0)
    weight = weight[...].reshape(6 * ch, 2 * ch)
    both = jnp.dot(window, weight, preferred_element_type=jnp.float32)
    results, start = [], 0
    for part in windows:
        end = start + part.shape[0]
        results.append(both[start + cols : end, :ch] + both[start : end - cols, ch:])
        start = end
    return results


def paired(source, target, sem):
    ch = source.shape[-1]
    return [
        pltpu.make_async_copy(source.at[pl.ds(1, 2)], target.at[:, :, :, :ch], sem.at[0]),
        pltpu.make_async_copy(source.at[0], target.at[0, :, :, ch:], sem.at[1]),
    ]


def above_and_below(upper, lower, rim, has_up, has_down):
    upper = jnp.concatenate([jnp.where(has_up, upper[:rim], 0.0), upper[rim:]], axis=0)
    lower = jnp.concatenate([lower[:-rim], jnp.where(has_down, lower[-rim:], 0.0)], axis=0)
    return upper, lower


def kernel(
    frames, rows_devices,
    feat, w_in, b_in_hbm, w_mid, b_mid_hbm, w_out, b_out_hbm,
    out_f, out_b,
    fields, state, pre, inner, wf, ws, wm, wo, b_in, b_mid, b_out,
    load_sem, bias_sem, feat_send, feat_recv, first_send, rim_send, rim_recv,
    state_send, state_recv, out_send, out_recv,
):
    z = lax.axis_index("frame")
    r = lax.axis_index("row")
    clips, _, rows, cols, ch = feat.shape
    span = rows + 2 * HALO
    has_up, has_down = r > 0, r < rows_devices - 1
    own = pl.ds(HALO, rows)
    sides = (
        (has_up, -1, 0, HALO + rows),
        (has_down, 1, rows - HALO, 0),
    )

    back = jnp.where(z >= frames - clips, 1, 0)
    clip = z + back * (frames - 1 - 2 * z)
    is_host = (z < clips) | (z >= frames - clips)

    def host_of(k, c):
        return c + k * (frames - 1 - 2 * c)

    def frame_of(s):
        return s + back * (frames - 1 - 2 * s)

    barrier = pltpu.get_barrier_semaphore()
    near = [(z != zz, zz, r) for zz in range(frames)]
    for near_row, offset, _, _ in sides:
        for dz in (-1, 0, 1):
            near.append((near_row & (z + dz >= 0) & (z + dz < frames), z + dz, r + offset))
    for ok, zz, rr in near:
        @pl.when(ok)
        def _(zz=zz, rr=rr):
            pl.semaphore_signal(barrier, inc=1, device_id={"frame": zz, "row": rr})

    weights = (
        (w_in.at[back, :, :, :ch], wf),
        (w_in.at[back, :, :, ch:], ws),
        (w_mid.at[back], wm),
        (w_out.at[back], wo),
    )
    loads = []
    for i, (source, target) in enumerate(weights):
        loads += paired(source, target, load_sem.at[i])
    biases = ((b_in_hbm, b_in), (b_mid_hbm, b_mid), (b_out_hbm, b_out))
    for i, (source, target) in enumerate(biases):
        loads.insert(2 + i, pltpu.make_async_copy(source, target, bias_sem.at[i]))
    for load in loads:
        load.start()
    for _, target in weights:
        target[1, :, :, ch:] = jnp.zeros((3, ch, ch), jnp.bfloat16)

    for near_row, _, _, keep in sides:
        at = HALO + rows - keep
        @pl.when(jnp.logical_not(near_row))
        def _(at=at):
            zeros = jnp.zeros((frames, HALO, cols, ch), jnp.bfloat16)
            fields[:, at : at + HALO] = zeros
            state[:, at : at + HALO] = zeros

    pl.semaphore_wait(barrier, sum(jnp.where(ok, 1, 0) for ok, _, _ in near))

    late = jnp.where(2 * z >= frames, 1, 0)

    def feature_copy(i):
        half = i // clips
        k = late + half - 2 * late * half
        c = i % clips
        host = host_of(k, c)
        copy = pltpu.make_async_remote_copy(
            feat.at[c, 0], fields.at[z, own], feat_send.at[i], feat_recv.at[z],
            device_id={"frame": host},
        )
        return c, host, copy

    def first_rims(c):
        host = host_of(back, c)
        is_first = (z == 0) | (z == frames - 1)
        return [
            (
                is_first & near_row,
                pltpu.make_async_remote_copy(
                    feat.at[c, 0, pl.ds(take, HALO)], fields.at[z, pl.ds(keep, HALO)],
                    first_send.at[c, side], rim_recv.at[z, side],
                    device_id={"frame": host, "row": r + offset},
                ),
            )
            for side, (near_row, offset, take, keep) in enumerate(sides)
        ]

    for i in range(2 * clips):
        c, host, copy = feature_copy(i)
        pl.when(host != z)(copy.start)
        @pl.when(host == z)
        def _(c=c):
            pltpu.make_async_copy(feat.at[c, 0], fields.at[z, own], feat_recv.at[z]).start()
        if i < clips:
            for ok, copy in first_rims(i):
                pl.when(ok)(copy.start)

    def rim_copies(buffer, index, sends, gets):
        made = []
        for side, (near_row, offset, take, keep) in enumerate(sides):
            copy = pltpu.make_async_remote_copy(
                buffer.at[index, pl.ds(HALO + take, HALO)], buffer.at[index, pl.ds(keep, HALO)],
                sends.at[index, side], gets.at[index, side], device_id={"row": r + offset},
            )
            made.append((near_row, sides[1 - side][0], copy))
        return made

    def field_rims(f):
        return rim_copies(fields, f, rim_send, rim_recv)

    def state_rims(s):
        return rim_copies(state, s, state_send, state_recv)

    def wait_field(f):
        pltpu.make_async_copy(feat.at[0, 0], fields.at[f, own], feat_recv.at[f]).wait()

    def wait_rims(copies):
        for _, comes, copy in copies:
            pl.when(comes)(copy.wait_recv)

    def out_copy(s, k):
        return pltpu.make_async_remote_copy(
            state.at[s, own], (out_f, out_b)[k].at[clip, 0], out_send.at[s],
            out_recv.at[k, clip], device_id={"frame": frame_of(s)},
        )

    rim, wide = HALO * cols, (rows + 4) * cols

    def flat(block):
        return block.reshape(block.shape[0] * cols, ch).astype(jnp.float32)

    def rounded(values):
        return values.astype(jnp.bfloat16).astype(jnp.float32)

    def features_part(f):
        pre[...] = conv([flat(fields[f])], wf, cols)[0] + b_in[pl.ds(back, 1), :]

    def chain():
        wait_field(frame_of(0))
        for load in loads[:5]:
            load.wait()
        wait_rims(field_rims(frame_of(0)))
        features_part(frame_of(0))
        inner[...] = rounded(activate(pre[rim : wide - rim]))
        for load in loads[5:]:
            load.wait()

        def step(s, carry):
            f = frame_of(s)
            more = s < frames - 1
            then = frame_of(jnp.minimum(s + 1, frames - 1))

            @pl.when(more)
            def _():
                wait_field(then)
                for goes, _, copy in field_rims(then):
                    pl.when(goes)(copy.start)

            @pl.when(s > 0)
            def _():
                before = jnp.maximum(s - 1, 0)
                wait_rims(state_rims(before))
                ends = [flat(state[before, : HALO + 2]), flat(state[before, rows + 1 :])]
                upper, lower = conv(ends, ws, cols)
                pre[:rim] += upper
                pre[wide - rim :] += lower

            upper, lower = activate(pre[:rim]), activate(pre[wide - rim :])
            upper, lower = above_and_below(upper, lower, 2 * cols, has_up, has_down)
            first = jnp.concatenate([rounded(upper), inner[...], rounded(lower)], axis=0)
            mid = activate(conv([first], wm, cols)[0] + b_mid[pl.ds(back, 1), :])
            upper, lower = above_and_below(mid[:rim], mid[rim:], cols, has_up, has_down)
            mid = jnp.concatenate([upper, lower], axis=0)
            last = conv([mid], wo, cols)[0] + b_out[pl.ds(back, 1), :]
            new = first[2 * cols : (2 + rows) * cols] + last
            state[s, own] = new.astype(jnp.bfloat16).reshape(rows, cols, ch)

            for goes, _, copy in state_rims(s):
                pl.when(goes & more)(copy.start)
            for k in range(2):
                pl.when((back == k) & (f != z))(out_copy(s, k).start)
                @pl.when((back == k) & (f == z))
                def _(k=k):
                    pltpu.make_async_copy(
                        state.at[s, own], (out_f, out_b)[k].at[clip, 0], out_recv.at[k, clip]
                    ).start()

            @pl.when(more)
            def _():
                wait_rims(field_rims(then))
                features_part(then)
                part = conv([flat(state[s, own])], ws, cols)[0]
                inner[...] = rounded(activate(pre[rim : wide - rim] + part))

            return carry

        lax.fori_loop(0, frames, step, 0)

        for s in range(frames):
            f = frame_of(s)
            pl.when(f != z)(out_copy(s, 0).wait_send)
            if s < frames - 1:
                for goes, _, copy in state_rims(s):
                    pl.when(goes)(copy.wait_send)
            if s > 0:
                for goes, _, copy in field_rims(f):
                    pl.when(goes)(copy.wait_send)

    if frames == 2 * clips:
        chain()
    else:
        pl.when(is_host)(chain)
        @pl.when(jnp.logical_not(is_host))
        def _():
            for load in loads:
                load.wait()

    for i in range(2 * clips):
        _, host, copy = feature_copy(i)
        pl.when(host != z)(copy.wait_send)
    for c in range(clips):
        for ok, copy in first_rims(c):
            pl.when(ok)(copy.wait_send)
        for k, out in enumerate((out_f, out_b)):
            pltpu.make_async_copy(state.at[0, own], out.at[c, 0], out_recv.at[k, c]).wait()


def on_device(features, w_in, b_in, w_mid, b_mid, w_out, b_out):
    clips, held, rows, cols, ch = features.shape
    frames = lax.axis_size("frame")
    assert held == 1 and rows >= HALO and clips <= 2 and frames >= 2 * clips
    span = rows + 2 * HALO
    bf16 = jnp.bfloat16
    hbm = pl.BlockSpec(memory_space=pltpu.HBM)
    dma = pltpu.SemaphoreType.DMA
    return pl.pallas_call(
        functools.partial(kernel, frames, lax.axis_size("row")),
        out_shape=[pltpu.VMEM(features.shape, bf16)] * 2,
        in_specs=[hbm] * 7,
        out_specs=[pl.BlockSpec(memory_space=pl.ANY)] * 2,
        scratch_shapes=[
            pltpu.VMEM((frames, span, cols, ch), bf16),
            pltpu.VMEM((frames, span, cols, ch), bf16),
            pltpu.VMEM(((rows + 4) * cols, ch), jnp.float32),
            pltpu.VMEM(((rows - 2) * cols, ch), jnp.float32),
            pltpu.VMEM((2, 3, ch, 2 * ch), bf16),
            pltpu.VMEM((2, 3, ch, 2 * ch), bf16),
            pltpu.VMEM((2, 3, ch, 2 * ch), bf16),
            pltpu.VMEM((2, 3, ch, 2 * ch), bf16),
            pltpu.VMEM((2, ch), jnp.float32),
            pltpu.VMEM((2, ch), jnp.float32),
            pltpu.VMEM((2, ch), jnp.float32),
            dma((4, 2)),
            dma((3,)),
            dma((2 * clips,)),
            dma((frames,)),
            dma((clips, 2)),
            dma((frames, 2)),
            dma((frames, 2)),
            dma((frames, 2)),
            dma((frames, 2)),
            dma((frames,)),
            dma((2, clips)),
        ],
        compiler_params=pltpu.CompilerParams(
            collective_id=0, has_side_effects=True, vmem_limit_bytes=60 * 1024 * 1024
        ),
    )(features, w_in, b_in, w_mid, b_mid, w_out, b_out)


def solution(mesh):
    split = P("parts", "frame", "row", None, None)
    return jax.shard_map(
        on_device,
        mesh=mesh,
        in_specs=(split, P(), P(), P(), P(), P(), P()),
        out_specs=(split, split),
        check_vma=False,
    )
```

```python
import functools

import jax
import jax.numpy as jnp
from jax import lax
from jax.experimental import pallas as pl
from jax.experimental.pallas import tpu as pltpu
from jax.sharding import PartitionSpec as P

HALO = 3


def activate(values):
    return 0.5 * values * (lax.erf(values * (0.5**0.5)) + 1.0)


def side_taps(values, cols):
    count, ch = values.shape
    col = lax.broadcasted_iota(jnp.int32, (1, cols, ch), 1)

    def beside(by, edge):
        moved = pltpu.roll(values, by, 0).reshape(count // cols, cols, ch)
        return jnp.where(col == edge, 0.0, moved).reshape(count, ch)

    left, right = beside(1, 0), beside(count - 1, cols - 1)
    return jnp.concatenate([left, values, right], axis=1).astype(jnp.bfloat16)


def conv(fields, weight, cols):
    ch = fields[0].shape[1]
    taps = [side_taps(field, cols) for field in fields]
    windows = [jnp.concatenate([tap[:-cols], tap[cols:]], axis=1) for tap in taps]
    window = windows[0] if len(windows) == 1 else jnp.concatenate(windows, axis=0)
    weight = weight[...].reshape(6 * ch, 2 * ch)
    both = jnp.dot(window, weight, preferred_element_type=jnp.float32)
    results, start = [], 0
    for part in windows:
        end = start + part.shape[0]
        results.append(both[start + cols : end, :ch] + both[start : end - cols, ch:])
        start = end
    return results


def paired(source, target, sem):
    ch = source.shape[-1]
    return [
        pltpu.make_async_copy(source.at[pl.ds(1, 2)], target.at[:, :, :, :ch], sem.at[0]),
        pltpu.make_async_copy(source.at[0], target.at[0, :, :, ch:], sem.at[1]),
    ]


def above_and_below(upper, lower, rim, has_up, has_down):
    upper = jnp.concatenate([jnp.where(has_up, upper[:rim], 0.0), upper[rim:]], axis=0)
    lower = jnp.concatenate([lower[:-rim], jnp.where(has_down, lower[-rim:], 0.0)], axis=0)
    return upper, lower


def kernel(
    frames, rows_devices,
    feat, w_in, b_in_hbm, w_mid, b_mid_hbm, w_out, b_out_hbm,
    out_f, out_b,
    fields, state, pre, inner, wf, ws, wm, wo, b_in, b_mid, b_out,
    load_sem, bias_sem, feat_send, feat_recv, first_send, rim_send, rim_recv,
    state_send, state_recv, out_send, out_recv,
):
    z = lax.axis_index("frame")
    r = lax.axis_index("row")
    clips, _, rows, cols, ch = feat.shape
    span = rows + 2 * HALO
    has_up, has_down = r > 0, r < rows_devices - 1
    own = pl.ds(HALO, rows)
    sides = (
        (has_up, -1, 0, HALO + rows),
        (has_down, 1, rows - HALO, 0),
    )

    back = jnp.where(z >= frames - clips, 1, 0)
    clip = z + back * (frames - 1 - 2 * z)
    is_host = (z < clips) | (z >= frames - clips)

    def host_of(k, c):
        return c + k * (frames - 1 - 2 * c)

    def frame_of(s):
        return s + back * (frames - 1 - 2 * s)

    barrier = pltpu.get_barrier_semaphore()
    near = [(z != zz, zz, r) for zz in range(frames)]
    for near_row, offset, _, _ in sides:
        for dz in (-1, 0, 1):
            near.append((near_row & (z + dz >= 0) & (z + dz < frames), z + dz, r + offset))
    for ok, zz, rr in near:
        @pl.when(ok)
        def _(zz=zz, rr=rr):
            pl.semaphore_signal(barrier, inc=1, device_id={"frame": zz, "row": rr})

    weights = (
        (w_in.at[back, :, :, :ch], wf),
        (w_in.at[back, :, :, ch:], ws),
        (w_mid.at[back], wm),
        (w_out.at[back], wo),
    )
    loads = []
    for i, (source, target) in enumerate(weights):
        loads += paired(source, target, load_sem.at[i])
    biases = ((b_in_hbm, b_in), (b_mid_hbm, b_mid), (b_out_hbm, b_out))
    for i, (source, target) in enumerate(biases):
        loads.insert(2 + i, pltpu.make_async_copy(source, target, bias_sem.at[i]))
    for load in loads:
        load.start()
    for _, target in weights:
        target[1, :, :, ch:] = jnp.zeros((3, ch, ch), jnp.bfloat16)

    for near_row, _, _, keep in sides:
        at = HALO + rows - keep
        @pl.when(jnp.logical_not(near_row))
        def _(at=at):
            zeros = jnp.zeros((frames, HALO, cols, ch), jnp.bfloat16)
            fields[:, at : at + HALO] = zeros
            state[:, at : at + HALO] = zeros

    pl.semaphore_wait(barrier, sum(jnp.where(ok, 1, 0) for ok, _, _ in near))

    late = jnp.where(2 * z >= frames, 1, 0)

    def feature_copy(i):
        half = i // clips
        k = late + half - 2 * late * half
        c = i % clips
        host = host_of(k, c)
        copy = pltpu.make_async_remote_copy(
            feat.at[c, 0], fields.at[z, own], feat_send.at[i], feat_recv.at[z],
            device_id={"frame": host},
        )
        return c, host, copy

    def first_rims(c):
        host = host_of(back, c)
        is_first = (z == 0) | (z == frames - 1)
        return [
            (
                is_first & near_row,
                pltpu.make_async_remote_copy(
                    feat.at[c, 0, pl.ds(take, HALO)], fields.at[z, pl.ds(keep, HALO)],
                    first_send.at[c, side], rim_recv.at[z, side],
                    device_id={"frame": host, "row": r + offset},
                ),
            )
            for side, (near_row, offset, take, keep) in enumerate(sides)
        ]

    def send_feature(i):
        c, host, copy = feature_copy(i)
        pl.when(host != z)(copy.start)
        @pl.when(host == z)
        def _():
            pltpu.make_async_copy(feat.at[c, 0], fields.at[z, own], feat_recv.at[z]).start()

    def send_later():
        for i in range(clips, 2 * clips):
            send_feature(i)

    for c in range(clips):
        for ok, copy in first_rims(c):
            pl.when(ok)(copy.start)
        send_feature(c)

    def rim_copies(buffer, index, sends, gets):
        made = []
        for side, (near_row, offset, take, keep) in enumerate(sides):
            copy = pltpu.make_async_remote_copy(
                buffer.at[index, pl.ds(HALO + take, HALO)], buffer.at[index, pl.ds(keep, HALO)],
                sends.at[index, side], gets.at[index, side], device_id={"row": r + offset},
            )
            made.append((near_row, sides[1 - side][0], copy))
        return made

    def field_rims(f):
        return rim_copies(fields, f, rim_send, rim_recv)

    def state_rims(s):
        return rim_copies(state, s, state_send, state_recv)

    def wait_field(f):
        pltpu.make_async_copy(feat.at[0, 0], fields.at[f, own], feat_recv.at[f]).wait()

    def wait_rims(copies):
        for _, comes, copy in copies:
            pl.when(comes)(copy.wait_recv)

    def out_copy(s, k):
        return pltpu.make_async_remote_copy(
            state.at[s, own], (out_f, out_b)[k].at[clip, 0], out_send.at[s],
            out_recv.at[k, clip], device_id={"frame": frame_of(s)},
        )

    rim, wide = HALO * cols, (rows + 4) * cols

    def flat(block):
        return block.reshape(block.shape[0] * cols, ch).astype(jnp.float32)

    def rounded(values):
        return values.astype(jnp.bfloat16).astype(jnp.float32)

    def features_part(f):
        pre[...] = conv([flat(fields[f])], wf, cols)[0] + b_in[pl.ds(back, 1), :]

    def chain():
        wait_field(frame_of(0))
        for load in loads[:5]:
            load.wait()
        wait_rims(field_rims(frame_of(0)))
        send_later()
        features_part(frame_of(0))
        inner[...] = rounded(activate(pre[rim : wide - rim]))
        for load in loads[5:]:
            load.wait()

        def step(s, carry):
            f = frame_of(s)
            more = s < frames - 1
            then = frame_of(jnp.minimum(s + 1, frames - 1))

            @pl.when(s > 0)
            def _():
                before = jnp.maximum(s - 1, 0)
                wait_rims(state_rims(before))
                ends = [flat(state[before, : HALO + 2]), flat(state[before, rows + 1 :])]
                upper, lower = conv(ends, ws, cols)
                pre[:rim] += upper
                pre[wide - rim :] += lower

            @pl.when(more)
            def _():
                wait_field(then)
                for goes, _, copy in field_rims(then):
                    pl.when(goes)(copy.start)

            upper, lower = activate(pre[:rim]), activate(pre[wide - rim :])
            upper, lower = above_and_below(upper, lower, 2 * cols, has_up, has_down)
            first = jnp.concatenate([rounded(upper), inner[...], rounded(lower)], axis=0)
            mid = activate(conv([first], wm, cols)[0] + b_mid[pl.ds(back, 1), :])
            upper, lower = above_and_below(mid[:rim], mid[rim:], cols, has_up, has_down)
            mid = jnp.concatenate([upper, lower], axis=0)
            last = conv([mid], wo, cols)[0] + b_out[pl.ds(back, 1), :]
            new = first[2 * cols : (2 + rows) * cols] + last
            state[s, own] = new.astype(jnp.bfloat16).reshape(rows, cols, ch)

            for goes, _, copy in state_rims(s):
                pl.when(goes & more)(copy.start)
            for k in range(2):
                pl.when((back == k) & (f != z))(out_copy(s, k).start)
                @pl.when((back == k) & (f == z))
                def _(k=k):
                    pltpu.make_async_copy(
                        state.at[s, own], (out_f, out_b)[k].at[clip, 0], out_recv.at[k, clip]
                    ).start()

            @pl.when(more)
            def _():
                wait_rims(field_rims(then))
                features_part(then)
                part = conv([flat(state[s, own])], ws, cols)[0]
                inner[...] = rounded(activate(pre[rim : wide - rim] + part))

            return carry

        lax.fori_loop(0, frames, step, 0)

        for s in range(frames):
            f = frame_of(s)
            pl.when(f != z)(out_copy(s, 0).wait_send)
            if s < frames - 1:
                for goes, _, copy in state_rims(s):
                    pl.when(goes)(copy.wait_send)
            if s > 0:
                for goes, _, copy in field_rims(f):
                    pl.when(goes)(copy.wait_send)

    if frames == 2 * clips:
        chain()
    else:
        pl.when(is_host)(chain)
        @pl.when(jnp.logical_not(is_host))
        def _():
            send_later()
            for load in loads:
                load.wait()

    for i in range(2 * clips):
        _, host, copy = feature_copy(i)
        pl.when(host != z)(copy.wait_send)
    for c in range(clips):
        for ok, copy in first_rims(c):
            pl.when(ok)(copy.wait_send)
        for k, out in enumerate((out_f, out_b)):
            pltpu.make_async_copy(state.at[0, own], out.at[c, 0], out_recv.at[k, c]).wait()


def on_device(features, w_in, b_in, w_mid, b_mid, w_out, b_out):
    clips, held, rows, cols, ch = features.shape
    frames = lax.axis_size("frame")
    assert held == 1 and rows >= HALO and clips <= 2 and frames >= 2 * clips
    span = rows + 2 * HALO
    bf16 = jnp.bfloat16
    hbm = pl.BlockSpec(memory_space=pltpu.HBM)
    dma = pltpu.SemaphoreType.DMA
    return pl.pallas_call(
        functools.partial(kernel, frames, lax.axis_size("row")),
        out_shape=[pltpu.VMEM(features.shape, bf16)] * 2,
        in_specs=[hbm] * 7,
        out_specs=[pl.BlockSpec(memory_space=pl.ANY)] * 2,
        scratch_shapes=[
            pltpu.VMEM((frames, span, cols, ch), bf16),
            pltpu.VMEM((frames, span, cols, ch), bf16),
            pltpu.VMEM(((rows + 4) * cols, ch), jnp.float32),
            pltpu.VMEM(((rows - 2) * cols, ch), jnp.float32),
            pltpu.VMEM((2, 3, ch, 2 * ch), bf16),
            pltpu.VMEM((2, 3, ch, 2 * ch), bf16),
            pltpu.VMEM((2, 3, ch, 2 * ch), bf16),
            pltpu.VMEM((2, 3, ch, 2 * ch), bf16),
            pltpu.VMEM((2, ch), jnp.float32),
            pltpu.VMEM((2, ch), jnp.float32),
            pltpu.VMEM((2, ch), jnp.float32),
            dma((4, 2)),
            dma((3,)),
            dma((2 * clips,)),
            dma((frames,)),
            dma((clips, 2)),
            dma((frames, 2)),
            dma((frames, 2)),
            dma((frames, 2)),
            dma((frames, 2)),
            dma((frames,)),
            dma((2, clips)),
        ],
        compiler_params=pltpu.CompilerParams(
            collective_id=0, has_side_effects=True, vmem_limit_bytes=60 * 1024 * 1024
        ),
    )(features, w_in, b_in, w_mid, b_mid, w_out, b_out)


def solution(mesh):
    split = P("parts", "frame", "row", None, None)
    return jax.shard_map(
        on_device,
        mesh=mesh,
        in_specs=(split, P(), P(), P(), P(), P(), P()),
        out_specs=(split, split),
        check_vma=False,
    )
```

```python
import functools

import jax
import jax.numpy as jnp
from jax import lax
from jax.experimental import pallas as pl
from jax.experimental.pallas import tpu as pltpu
from jax.sharding import PartitionSpec as P

HALO = 3


def activate(values):
    return 0.5 * values * (lax.erf(values * (0.5**0.5)) + 1.0)


def side_taps(values, cols):
    count, ch = values.shape
    col = lax.broadcasted_iota(jnp.int32, (1, cols, ch), 1)

    def beside(by, edge):
        moved = pltpu.roll(values, by, 0).reshape(count // cols, cols, ch)
        return jnp.where(col == edge, 0.0, moved).reshape(count, ch)

    left, right = beside(1, 0), beside(count - 1, cols - 1)
    return jnp.concatenate([left, values, right], axis=1).astype(jnp.bfloat16)


def conv(fields, weight, cols):
    ch = fields[0].shape[1]
    taps = [side_taps(field, cols) for field in fields]
    windows = [jnp.concatenate([tap[:-cols], tap[cols:]], axis=1) for tap in taps]
    window = windows[0] if len(windows) == 1 else jnp.concatenate(windows, axis=0)
    weight = weight[...].reshape(6 * ch, 2 * ch)
    both = jnp.dot(window, weight, preferred_element_type=jnp.float32)
    results, start = [], 0
    for part in windows:
        end = start + part.shape[0]
        results.append(both[start + cols : end, :ch] + both[start : end - cols, ch:])
        start = end
    return results


def paired(source, target, sem):
    ch = source.shape[-1]
    return [
        pltpu.make_async_copy(source.at[pl.ds(1, 2)], target.at[:, :, :, :ch], sem.at[0]),
        pltpu.make_async_copy(source.at[0], target.at[0, :, :, ch:], sem.at[1]),
    ]


def above_and_below(upper, lower, rim, has_up, has_down):
    upper = jnp.concatenate([jnp.where(has_up, upper[:rim], 0.0), upper[rim:]], axis=0)
    lower = jnp.concatenate([lower[:-rim], jnp.where(has_down, lower[-rim:], 0.0)], axis=0)
    return upper, lower


def kernel(
    frames, rows_devices,
    feat, w_in, b_in_hbm, w_mid, b_mid_hbm, w_out, b_out_hbm,
    out_f, out_b,
    fields, state, pre, inner, wf, ws, wm, wo, b_in, b_mid, b_out,
    load_sem, bias_sem, feat_send, feat_recv, first_send, rim_send, rim_recv,
    state_send, state_recv, out_send, out_recv,
):
    z = lax.axis_index("frame")
    r = lax.axis_index("row")
    clips, _, rows, cols, ch = feat.shape
    span = rows + 2 * HALO
    has_up, has_down = r > 0, r < rows_devices - 1
    own = pl.ds(HALO, rows)
    sides = (
        (has_up, -1, 0, HALO + rows),
        (has_down, 1, rows - HALO, 0),
    )

    back = jnp.where(z >= frames - clips, 1, 0)
    clip = z + back * (frames - 1 - 2 * z)
    is_host = (z < clips) | (z >= frames - clips)

    def host_of(k, c):
        return c + k * (frames - 1 - 2 * c)

    def frame_of(s):
        return s + back * (frames - 1 - 2 * s)

    barrier = pltpu.get_barrier_semaphore()
    near = [(z != zz, zz, r) for zz in range(frames)]
    for near_row, offset, _, _ in sides:
        for dz in (-1, 0, 1):
            near.append((near_row & (z + dz >= 0) & (z + dz < frames), z + dz, r + offset))
    for ok, zz, rr in near:
        @pl.when(ok)
        def _(zz=zz, rr=rr):
            pl.semaphore_signal(barrier, inc=1, device_id={"frame": zz, "row": rr})

    weights = (
        (w_in.at[back, :, :, :ch], wf),
        (w_in.at[back, :, :, ch:], ws),
        (w_mid.at[back], wm),
        (w_out.at[back], wo),
    )
    loads = []
    for i, (source, target) in enumerate(weights):
        loads += paired(source, target, load_sem.at[i])
    biases = ((b_in_hbm, b_in), (b_mid_hbm, b_mid), (b_out_hbm, b_out))
    for i, (source, target) in enumerate(biases):
        loads.insert(2 + i, pltpu.make_async_copy(source, target, bias_sem.at[i]))
    for load in loads:
        load.start()
    for _, target in weights:
        target[1, :, :, ch:] = jnp.zeros((3, ch, ch), jnp.bfloat16)

    for near_row, _, _, keep in sides:
        at = HALO + rows - keep
        @pl.when(jnp.logical_not(near_row))
        def _(at=at):
            zeros = jnp.zeros((frames, HALO, cols, ch), jnp.bfloat16)
            fields[:, at : at + HALO] = zeros
            state[:, at : at + HALO] = zeros

    pl.semaphore_wait(barrier, sum(jnp.where(ok, 1, 0) for ok, _, _ in near))

    late = jnp.where(2 * z >= frames, 1, 0)

    def feature_copy(i):
        half = i // clips
        k = late + half - 2 * late * half
        c = i % clips
        host = host_of(k, c)
        copy = pltpu.make_async_remote_copy(
            feat.at[c, 0], fields.at[z, own], feat_send.at[i], feat_recv.at[z],
            device_id={"frame": host},
        )
        return c, host, copy

    def first_rims(c):
        host = host_of(back, c)
        is_first = (z == 0) | (z == frames - 1)
        return [
            (
                is_first & near_row,
                pltpu.make_async_remote_copy(
                    feat.at[c, 0, pl.ds(take, HALO)], fields.at[z, pl.ds(keep, HALO)],
                    first_send.at[c, side], rim_recv.at[z, side],
                    device_id={"frame": host, "row": r + offset},
                ),
            )
            for side, (near_row, offset, take, keep) in enumerate(sides)
        ]

    for i in range(2 * clips):
        c, host, copy = feature_copy(i)
        pl.when(host != z)(copy.start)
        @pl.when(host == z)
        def _(c=c):
            pltpu.make_async_copy(feat.at[c, 0], fields.at[z, own], feat_recv.at[z]).start()
        if i < clips:
            for ok, copy in first_rims(i):
                pl.when(ok)(copy.start)

    def rim_copies(buffer, index, sends, gets):
        made = []
        for side, (near_row, offset, take, keep) in enumerate(sides):
            copy = pltpu.make_async_remote_copy(
                buffer.at[index, pl.ds(HALO + take, HALO)], buffer.at[index, pl.ds(keep, HALO)],
                sends.at[index, side], gets.at[index, side], device_id={"row": r + offset},
            )
            made.append((near_row, sides[1 - side][0], copy))
        return made

    def field_rims(f):
        return rim_copies(fields, f, rim_send, rim_recv)

    def state_rims(s):
        return rim_copies(state, s, state_send, state_recv)

    def wait_field(f):
        pltpu.make_async_copy(feat.at[0, 0], fields.at[f, own], feat_recv.at[f]).wait()

    def wait_rims(copies):
        for _, comes, copy in copies:
            pl.when(comes)(copy.wait_recv)

    def out_copy(s, k):
        return pltpu.make_async_remote_copy(
            state.at[s, own], (out_f, out_b)[k].at[clip, 0], out_send.at[s],
            out_recv.at[k, clip], device_id={"frame": frame_of(s)},
        )

    rim, wide = HALO * cols, (rows + 4) * cols

    def flat(block):
        return block.reshape(block.shape[0] * cols, ch).astype(jnp.float32)

    def rounded(values):
        return values.astype(jnp.bfloat16).astype(jnp.float32)

    def features_part(f):
        pre[...] = conv([flat(fields[f])], wf, cols)[0] + b_in[pl.ds(back, 1), :]

    def chain():
        wait_field(frame_of(0))
        for load in loads[:5]:
            load.wait()
        wait_rims(field_rims(frame_of(0)))
        features_part(frame_of(0))
        inner[...] = rounded(activate(pre[rim : wide - rim]))
        for load in loads[5:]:
            load.wait()

        def step(s, carry):
            f = frame_of(s)
            more = s < frames - 1
            then = frame_of(jnp.minimum(s + 1, frames - 1))

            @pl.when(more)
            def _():
                wait_field(then)
                for goes, _, copy in field_rims(then):
                    pl.when(goes)(copy.start)

            @pl.when(s > 0)
            def _():
                before = jnp.maximum(s - 1, 0)
                wait_rims(state_rims(before))
                ends = [flat(state[before, : HALO + 2]), flat(state[before, rows + 1 :])]
                upper, lower = conv(ends, ws, cols)
                pre[:rim] += upper
                pre[wide - rim :] += lower

            upper, lower = activate(pre[:rim]), activate(pre[wide - rim :])
            upper, lower = above_and_below(upper, lower, 2 * cols, has_up, has_down)
            first = jnp.concatenate([rounded(upper), inner[...], rounded(lower)], axis=0)
            mid = activate(conv([first], wm, cols)[0] + b_mid[pl.ds(back, 1), :])
            upper, lower = above_and_below(mid[:rim], mid[rim:], cols, has_up, has_down)
            mid = jnp.concatenate([upper, lower], axis=0)
            last = conv([mid], wo, cols)[0] + b_out[pl.ds(back, 1), :]
            new = first[2 * cols : (2 + rows) * cols] + last
            state[s, own] = new.astype(jnp.bfloat16).reshape(rows, cols, ch)

            for goes, _, copy in state_rims(s):
                pl.when(goes & more)(copy.start)
            for k in range(2):
                pl.when((back == k) & (f != z))(out_copy(s, k).start)
                @pl.when((back == k) & (f == z))
                def _(k=k):
                    pltpu.make_async_copy(
                        state.at[s, own], (out_f, out_b)[k].at[clip, 0], out_recv.at[k, clip]
                    ).start()

            @pl.when(more)
            def _():
                inner[...] = conv([flat(state[s, own])], ws, cols)[0]
                wait_rims(field_rims(then))
                features_part(then)
                inner[...] = rounded(activate(pre[rim : wide - rim] + inner[...]))

            return carry

        lax.fori_loop(0, frames, step, 0)

        for s in range(frames):
            f = frame_of(s)
            pl.when(f != z)(out_copy(s, 0).wait_send)
            if s < frames - 1:
                for goes, _, copy in state_rims(s):
                    pl.when(goes)(copy.wait_send)
            if s > 0:
                for goes, _, copy in field_rims(f):
                    pl.when(goes)(copy.wait_send)

    if frames == 2 * clips:
        chain()
    else:
        pl.when(is_host)(chain)
        @pl.when(jnp.logical_not(is_host))
        def _():
            for load in loads:
                load.wait()

    for i in range(2 * clips):
        _, host, copy = feature_copy(i)
        pl.when(host != z)(copy.wait_send)
    for c in range(clips):
        for ok, copy in first_rims(c):
            pl.when(ok)(copy.wait_send)
        for k, out in enumerate((out_f, out_b)):
            pltpu.make_async_copy(state.at[0, own], out.at[c, 0], out_recv.at[k, c]).wait()


def on_device(features, w_in, b_in, w_mid, b_mid, w_out, b_out):
    clips, held, rows, cols, ch = features.shape
    frames = lax.axis_size("frame")
    assert held == 1 and rows >= HALO and clips <= 2 and frames >= 2 * clips
    span = rows + 2 * HALO
    bf16 = jnp.bfloat16
    hbm = pl.BlockSpec(memory_space=pltpu.HBM)
    dma = pltpu.SemaphoreType.DMA
    return pl.pallas_call(
        functools.partial(kernel, frames, lax.axis_size("row")),
        out_shape=[pltpu.VMEM(features.shape, bf16)] * 2,
        in_specs=[hbm] * 7,
        out_specs=[pl.BlockSpec(memory_space=pl.ANY)] * 2,
        scratch_shapes=[
            pltpu.VMEM((frames, span, cols, ch), bf16),
            pltpu.VMEM((frames, span, cols, ch), bf16),
            pltpu.VMEM(((rows + 4) * cols, ch), jnp.float32),
            pltpu.VMEM(((rows - 2) * cols, ch), jnp.float32),
            pltpu.VMEM((2, 3, ch, 2 * ch), bf16),
            pltpu.VMEM((2, 3, ch, 2 * ch), bf16),
            pltpu.VMEM((2, 3, ch, 2 * ch), bf16),
            pltpu.VMEM((2, 3, ch, 2 * ch), bf16),
            pltpu.VMEM((2, ch), jnp.float32),
            pltpu.VMEM((2, ch), jnp.float32),
            pltpu.VMEM((2, ch), jnp.float32),
            dma((4, 2)),
            dma((3,)),
            dma((2 * clips,)),
            dma((frames,)),
            dma((clips, 2)),
            dma((frames, 2)),
            dma((frames, 2)),
            dma((frames, 2)),
            dma((frames, 2)),
            dma((frames,)),
            dma((2, clips)),
        ],
        compiler_params=pltpu.CompilerParams(
            collective_id=0, has_side_effects=True, vmem_limit_bytes=60 * 1024 * 1024
        ),
    )(features, w_in, b_in, w_mid, b_mid, w_out, b_out)


def solution(mesh):
    split = P("parts", "frame", "row", None, None)
    return jax.shard_map(
        on_device,
        mesh=mesh,
        in_specs=(split, P(), P(), P(), P(), P(), P()),
        out_specs=(split, split),
        check_vma=False,
    )
```
